32 devices in a mesh: dp: 8 (over y, x, core), tensor: 4 (over z).
Axes of the slice: x: 2, y: 2, z: 4, core: 2. Of those that a mesh axis runs over, the one named last changes fastest.
Arguments:
- d_out: bfloat16 [8, 512, 2560], P('dp', 'tensor'), may hold values from -12 to 12
- attn_out: bfloat16 [8, 512, 3072], P('dp', None, 'tensor'), may hold values from -6 to 6
- queries: bfloat16 [8, 512, 3072], P('dp', None, 'tensor'), may hold values from -40 to 40
- keys: bfloat16 [8, 512, 3072], P('dp', None, 'tensor'), may hold values from -4 to 4
- out_weight: bfloat16 [3072, 2560], P('tensor'), may hold values from -0.125 to 0.125
- segment_ids: int32 [8, 512], P('dp'), may hold values from 0 to 1, as said below
Outputs:
- value_grad: bfloat16 [8, 512, 3072], P('dp', None, 'tensor')
- weight_grad: float32 [3072, 2560], P(('tensor', 'dp'))
The draws below stay inside these ranges and needn't reach their ends.
Inputs may be any that keep to these rules, and one draw needn't show every extreme that they name: `segment_ids`: ids start at 0, never fall along a sequence, and rise by one where a new document begins; exactly one new document begins in every aligned block of min(512, 512) positions.
All inputs are finite; a program needn't handle non-finite values.
Results may differ from the reference program's by a relative error of at most 0.008.
Values may be sent and summed in bfloat16 or wider, within the bound.
A program may use at most 64 MiB of HBM per device.

```python
import jax
import jax.numpy as jnp
from jax import lax

D = 2560
HEADS = 24
HEAD_DIM = 128
L = 512
SEQS = 8
ATTN_WIDTH = 3072


def common_draw(key):
    block_len = min(512, L)
    block_count = L // block_len
    offset_any = jax.random.randint(jax.random.fold_in(key, 101), (SEQS, block_count), 0, block_len)
    offset_first = jax.random.randint(jax.random.fold_in(key, 111), (SEQS, block_count), 1, block_len)
    block_index = jnp.arange(block_count)[None, :]
    offsets = jnp.where(block_index == 0, offset_first, offset_any)
    inside = jnp.arange(block_len)[None, None, :]
    starts = (inside == offsets[:, :, None]).reshape(SEQS, L)
    segments = jnp.cumsum(starts.astype(jnp.int32), axis=1).astype(jnp.int32)
    seed_query = jax.random.fold_in(key, 202)
    seed_keys = jax.random.fold_in(key, 303)
    shape_heads = (SEQS, L, HEADS, HEAD_DIM)
    query_full = jnp.clip(jax.random.normal(seed_query, shape_heads, jnp.float32), -4.0, 4.0)
    key_full = jnp.clip(jax.random.normal(seed_keys, shape_heads, jnp.float32), -4.0, 4.0)
    width_all = HEADS * HEAD_DIM
    return (segments, query_full.reshape(SEQS, L, width_all), key_full.reshape(SEQS, L, width_all))


def draw_segment_ids(key, part):
    return common_draw(key)[0]


def draw_queries(key, part):
    return common_draw(key)[1].astype(jnp.bfloat16)


def draw_keys(key, part):
    return common_draw(key)[2].astype(jnp.bfloat16)


def spiked(drawn, key, source, target, parts, factor):
    def block_of(axis_at):
        return (jnp.arange(drawn.shape[axis_at]) // (drawn.shape[axis_at] // parts)).reshape((-1,) + (1,) * (drawn.ndim - 1 - axis_at))

    near = jax.random.permutation(key, parts)[block_of(target)]
    far = (block_of(target) + parts // 2) % parts
    return jnp.where((block_of(source) == near) | (block_of(source) == far), factor * drawn, drawn)


def shard_levels(rng, shape, pieces, least, largest):
    loudness, own = 1.0, jax.random.fold_in(rng, 6)
    for dim, parts in pieces:
        heights = jnp.exp(jax.random.uniform(jax.random.fold_in(own, dim), (parts,), jnp.float32, least / len(pieces), largest / len(pieces)))
        loudness = loudness * jnp.repeat(heights, shape[dim] // parts).reshape([-1 if axis == dim else 1 for axis in range(len(shape))])
    return loudness


def centred(own_key, extent, deviation, most, pieces=(), kind=jnp.bfloat16):
    drawn = jax.random.normal(own_key, extent, jnp.float32) * deviation
    if len(pieces) > 0:
        drawn = shard_levels(own_key, extent, pieces, -0.22, 0.18) * drawn
    return jnp.clip(drawn, min=-most, max=most).astype(kind)


def heavy_noise(key, shape, deviation, most, shards, heavy, held_as=jnp.bfloat16):
    array = deviation * jax.random.normal(key, shape, jnp.float32)
    if shards:
        array = array * shard_levels(key, shape, shards, -0.22, 0.18)
    return jnp.clip(spiked(array, jax.random.fold_in(key, 3), *heavy), -most, most).astype(held_as)


def setup_inputs(seed: int = 0) -> dict:
    key_of = jax.random.split(jax.random.key(seed), 7)
    d_out = centred(key_of[0], (SEQS, L, D), 2.0, 12.0, ((0, 8), (1, 4)))
    attn_out = heavy_noise(key_of[1], (SEQS, L, ATTN_WIDTH), 1.0, 6.0, ((0, 8), (2, 4)), (0, 2, 8, 2.0))
    queries = draw_queries(jax.random.fold_in(key_of[6], 71), 0)
    keys = draw_keys(jax.random.fold_in(key_of[6], 71), 0)
    out_weight = centred(key_of[4], (ATTN_WIDTH, D), D ** -0.5, 0.125, ((0, 4),))
    segment_ids = draw_segment_ids(jax.random.fold_in(key_of[6], 71), 0)
    return dict(d_out=d_out, attn_out=attn_out, queries=queries, keys=keys, out_weight=out_weight, segment_ids=segment_ids)


def value_path(attn_grad, query_rows, key_rows, segment_row):
    query_heads = query_rows.astype(jnp.float32).reshape(L, HEADS, HEAD_DIM)
    key_heads = key_rows.astype(jnp.float32).reshape(L, HEADS, HEAD_DIM)
    scores = jnp.einsum("qhd,khd->hqk", query_heads, key_heads) * (HEAD_DIM ** -0.5)
    position = jnp.arange(L)
    allowed = (position[:, None] >= position[None, :]) & (segment_row[:, None] == segment_row[None, :])
    masked = jnp.where(allowed[None], scores, -jnp.inf)
    highest = jnp.max(masked, axis=2, keepdims=True)
    weights = jnp.where(allowed[None], jnp.exp(masked - highest), 0.0)
    probabilities = (weights / jnp.sum(weights, axis=2, keepdims=True)).astype(jnp.bfloat16)
    grad_heads = attn_grad.astype(jnp.float32).reshape(L, HEADS, HEAD_DIM)
    result = jnp.einsum("hqk,qhd->khd", probabilities.astype(jnp.float32), grad_heads)
    return result.reshape(L, HEADS * HEAD_DIM).astype(jnp.bfloat16)


def reference(d_out, attn_out, queries, keys, out_weight, segment_ids):
    def one_sequence(bucket_sum, sequence_items):
        grad_rows, output_rows, query_rows, key_rows, segment_row = sequence_items
        attn_grad = jnp.dot(grad_rows, out_weight.T, preferred_element_type=jnp.float32).astype(jnp.bfloat16)
        value_rows = value_path(attn_grad, query_rows, key_rows, segment_row)
        bucket_sum = bucket_sum + jnp.dot(output_rows.T, grad_rows, preferred_element_type=jnp.float32)
        return bucket_sum, value_rows

    start_sum = jnp.zeros((HEADS * HEAD_DIM, D), jnp.float32)
    bucket_sum, value_grad = lax.scan(one_sequence, start_sum, (d_out, attn_out, queries, keys, segment_ids))
    return value_grad, bucket_sum / SEQS
```

```python
import functools

import jax
import jax.numpy as jnp
from jax import lax
from jax.experimental import pallas as pl
from jax.experimental.pallas import tpu as pltpu
from jax.sharding import PartitionSpec as P

HEAD_DIM = 128


def value_path(queries, keys, attn_grad, segment_row):
    length = queries.shape[0]
    head_count = queries.shape[1] // HEAD_DIM
    query_heads = queries.reshape(length, head_count, HEAD_DIM)
    key_heads = keys.reshape(length, head_count, HEAD_DIM)
    grad_heads = attn_grad.reshape(length, head_count, HEAD_DIM)
    block_rows = min(256, length)
    score_scale = HEAD_DIM ** (-0.5)
    position = jnp.arange(length)
    result = jnp.zeros((length, head_count, HEAD_DIM), jnp.float32)
    for first_row in range(0, length, block_rows):
        stop_row = first_row + block_rows
        scores = (
            jnp.einsum(
                "qhd,khd->hqk",
                query_heads[first_row:stop_row],
                key_heads[:stop_row],
                preferred_element_type=jnp.float32,
            )
            * score_scale
        )
        allowed = (position[first_row:stop_row, None] >= position[None, :stop_row]) & (
            segment_row[first_row:stop_row, None] == segment_row[None, :stop_row]
        )
        masked = jnp.where(allowed[None], scores, -jnp.inf)
        highest = jnp.max(masked, axis=2, keepdims=True)
        weights = jnp.where(allowed[None], jnp.exp(masked - highest), 0.0)
        probabilities = (weights / jnp.sum(weights, axis=2, keepdims=True)).astype(jnp.bfloat16)
        update = jnp.einsum(
            "hqk,qhd->khd",
            probabilities,
            grad_heads[first_row:stop_row],
            preferred_element_type=jnp.float32,
        )
        result = result.at[:stop_row].add(update)
    return result.reshape(length, head_count * HEAD_DIM).astype(jnp.bfloat16)


def reduce_bucket(term_rows, owned_count):
    return lax.psum_scatter(
        term_rows(jnp.int32(0), owned_count * lax.axis_size("dp")),
        "dp",
        scatter_dimension=0,
        tiled=True,
    )


def fits_kernel(d_out, attn_out, out_weight):
    dp, tensor = lax.axis_size("dp"), lax.axis_size("tensor")
    rows, length = d_out.shape[1], attn_out.shape[1]
    features, width = out_weight.shape
    return (
        tensor >= 2
        and dp % 2 == 0
        and 4 <= dp <= 16
        and features % (dp * 16) == 0
        and features % HEAD_DIM == 0
        and rows % 16 == 0
        and length % 128 == 0
        and length * features * 24 + length * width * 2 + features * width * 7 < 40 * 2**20
        and width % chunk_width(width) == 0
        and width // chunk_width(width) >= 3
    )


def chunk_width(width):
    return 256 if width % 256 == 0 else 128


def kernel(
    dp,
    tensor,
    d_out,
    attn_out,
    queries,
    keys,
    weight,
    segments,
    value_out,
    owned_out,
    grads,
    weights,
    outputs,
    query_buf,
    key_buf,
    segment_buf,
    turned,
    flipped,
    probs,
    total,
    pair_send,
    pair_recv,
    kept,
    group_send,
    group_recv,
    mine,
    load_sem,
    grad_sem,
    weight_sem,
    up_send,
    up_recv,
    down_send,
    down_recv,
    pair_send_sem,
    pair_recv_sem,
    group_send_sem,
    group_recv_sem,
):
    chunks, length, width = grads.shape
    rows = length // tensor
    features = weight.shape[0]
    owned = features // dp
    groups = dp // 2
    heads = features // HEAD_DIM
    z = lax.axis_index("tensor")
    d = lax.axis_index("dp")
    core = lax.rem(d, 2)
    group = d // 2
    sibling = 2 * group + 1 - core
    last = chunks - 1

    def columns(c):
        return pl.ds(pl.multiple_of(c * width, width), width)

    def grad_rows(s):
        return pl.ds(pl.multiple_of(s * rows, rows), rows)

    def block_rows(g):
        return pl.ds(pl.multiple_of(g * owned, owned), owned)

    def load_grad(c):
        return pltpu.make_async_copy(
            d_out.at[0, :, columns(c)], grads.at[c, grad_rows(z), :], grad_sem.at[c]
        )

    def load_weight(c):
        return pltpu.make_async_copy(weight.at[:, columns(c)], weights.at[c], weight_sem.at[c])

    loads = [
        pltpu.make_async_copy(segments, segment_buf, load_sem.at[0]),
        pltpu.make_async_copy(queries.at[0], query_buf, load_sem.at[1]),
        pltpu.make_async_copy(keys.at[0], key_buf, load_sem.at[2]),
        pltpu.make_async_copy(attn_out.at[0], outputs, load_sem.at[3]),
    ]

    def start_grad(c, carry):
        load_grad(c).start()
        return carry

    def start_weight(c, carry):
        load_weight(c).start()
        return carry

    lax.fori_loop(0, chunks, start_grad, 0)
    for load in loads:
        load.start()
    lax.fori_loop(0, chunks, start_weight, 0)

    barrier = pltpu.get_barrier_semaphore()

    @pl.when(z > 0)
    def _():
        pl.semaphore_signal(barrier, inc=1, device_id={"tensor": z - 1}, device_id_type=pl.DeviceIdType.MESH)

    @pl.when(z < tensor - 1)
    def _():
        pl.semaphore_signal(barrier, inc=1, device_id={"tensor": z + 1}, device_id_type=pl.DeviceIdType.MESH)

    pl.semaphore_signal(barrier, inc=1, device_id={"dp": sibling}, device_id_type=pl.DeviceIdType.MESH)
    for step in range(1, groups):
        peer = 2 * lax.rem(group + step, groups) + core
        pl.semaphore_signal(barrier, inc=1, device_id={"dp": peer}, device_id_type=pl.DeviceIdType.MESH)

    pl.semaphore_wait(barrier, groups + jnp.minimum(z, 1) + jnp.minimum(tensor - 1 - z, 1))

    def up(c, hop):
        piece = grads.at[c, grad_rows(z - hop), :]
        return pltpu.make_async_remote_copy(
            src_ref=piece,
            dst_ref=piece,
            send_sem=up_send.at[hop, c],
            recv_sem=up_recv.at[hop, c],
            device_id={"tensor": z + 1},
            device_id_type=pl.DeviceIdType.MESH,
        )

    def down(c, hop):
        piece = grads.at[c, grad_rows(z + hop), :]
        return pltpu.make_async_remote_copy(
            src_ref=piece,
            dst_ref=piece,
            send_sem=down_send.at[hop, c],
            recv_sem=down_recv.at[hop, c],
            device_id={"tensor": z - 1},
            device_id_type=pl.DeviceIdType.MESH,
        )

    def arrived_up(c, hop):
        piece = grads.at[c, grad_rows(z - hop - 1), :]
        return pltpu.make_async_remote_copy(
            src_ref=piece,
            dst_ref=piece,
            send_sem=up_send.at[hop, c],
            recv_sem=up_recv.at[hop, c],
            device_id={"tensor": z - 1},
            device_id_type=pl.DeviceIdType.MESH,
        )

    def arrived_down(c, hop):
        piece = grads.at[c, grad_rows(z + hop + 1), :]
        return pltpu.make_async_remote_copy(
            src_ref=piece,
            dst_ref=piece,
            send_sem=down_send.at[hop, c],
            recv_sem=down_recv.at[hop, c],
            device_id={"tensor": z + 1},
            device_id_type=pl.DeviceIdType.MESH,
        )

    def send(c, hop):
        @pl.when((z - hop >= 0) & (z < tensor - 1))
        def _():
            up(c, hop).start()

        @pl.when((z + hop < tensor) & (z > 0))
        def _():
            down(c, hop).start()

    def send_own(c):
        load_grad(c).wait()
        send(c, 0)

    def receive(c, hop):
        @pl.when(z - hop - 1 >= 0)
        def _():
            arrived_up(c, hop).wait_recv()
            if hop + 1 < tensor - 1:

                @pl.when(z < tensor - 1)
                def _():
                    up(c, hop + 1).start()

        @pl.when(z + hop + 1 < tensor)
        def _():
            arrived_down(c, hop).wait_recv()
            if hop + 1 < tensor - 1:

                @pl.when(z > 0)
                def _():
                    down(c, hop + 1).start()

    def pair_copy(c):
        return pltpu.make_async_remote_copy(
            src_ref=pair_send.at[c],
            dst_ref=pair_recv.at[c],
            send_sem=pair_send_sem.at[c],
            recv_sem=pair_recv_sem.at[c],
            device_id={"dp": sibling},
            device_id_type=pl.DeviceIdType.MESH,
        )

    def group_copy(c, step):
        peer = 2 * lax.rem(group + step, groups) + core
        return pltpu.make_async_remote_copy(
            src_ref=group_send.at[c, step - 1],
            dst_ref=group_recv.at[c, step - 1],
            send_sem=group_send_sem.at[c, step - 1],
            recv_sem=group_recv_sem.at[c, step - 1],
            device_id={"dp": peer},
            device_id_type=pl.DeviceIdType.MESH,
        )

    ahead = min(2, chunks)
    for c in range(ahead):
        send_own(c)

    for load in loads:
        load.wait()
    turned[...] = outputs[...].T
    for part in range(2):
        owner_core = 1 - core if part == 0 else core
        for g in range(groups):
            flipped[part, g * owned : (g + 1) * owned, :] = turned[block_rows(2 * g + owner_core), :]
    total[...] = jnp.zeros_like(total)

    block = min(256, length)
    ids = segment_buf[...].astype(jnp.float32)
    ids_down = jnp.broadcast_to(ids, (128, length)).T[:, :1]

    def head_probs(h):
        at = pl.ds(pl.multiple_of(h * HEAD_DIM, HEAD_DIM), HEAD_DIM)
        for first in range(0, length, block):
            stop = first + block
            scores = lax.dot_general(
                key_buf[:stop, at],
                query_buf[first:stop, at],
                (((1,), (1,)), ((), ())),
                preferred_element_type=jnp.float32,
            ) * (HEAD_DIM ** (-0.5))
            key_at = lax.broadcasted_iota(jnp.int32, (stop, block), 0)
            query_at = first + lax.broadcasted_iota(jnp.int32, (stop, block), 1)
            allowed = (key_at <= query_at) & (ids_down[:stop] == ids[:, first:stop])
            masked = jnp.where(allowed, scores, -jnp.inf)
            highest = jnp.max(masked, axis=0, keepdims=True)
            terms = jnp.exp(masked - highest)
            probs[h, :stop, first:stop] = (
                terms * (1.0 / jnp.sum(terms, axis=0, keepdims=True))
            ).astype(jnp.bfloat16)

    def multiply(c):
        load_weight(c).wait()
        grad = grads[c]
        pair_send[c] = jnp.dot(flipped[0], grad, preferred_element_type=jnp.float32).astype(jnp.bfloat16)
        pair_copy(c).start()
        kept[c] = jnp.dot(flipped[1], grad, preferred_element_type=jnp.float32)
        total[...] += lax.dot_general(
            grad, weights[c], (((1,), (1,)), ((), ())), preferred_element_type=jnp.float32
        )

    def combine(c):
        pair_copy(c).wait_recv()
        for step in range(1, groups):
            at = block_rows(lax.rem(group + step, groups))
            group_send[c, step - 1] = (kept[c, at, :] + pair_recv[c, at, :].astype(jnp.float32)).astype(jnp.bfloat16)
            group_copy(c, step).start()
        at = block_rows(group)
        mine[c] = kept[c, at, :] + pair_recv[c, at, :].astype(jnp.float32)

    def finish(c):
        result = mine[c]
        for step in range(1, groups):
            group_copy(c, step).wait_recv()
            result += group_recv[c, step - 1].astype(jnp.float32)
        owned_out[:, columns(c)] = result / dp

    lag = tensor - 2

    def turn(k, carry):
        @pl.when(k + ahead < chunks)
        def _():
            send_own(k + ahead)

        @pl.when(k < heads)
        def _():
            head_probs(k)

        for hop in range(tensor - 1):
            c = k - hop

            @pl.when((c >= 0) & (c < chunks))
            def _():
                receive(c, hop)

        @pl.when(k - lag >= 0)
        def _():
            multiply(k - lag)

        @pl.when(k - lag - 1 >= 0)
        def _():
            combine(k - lag - 1)

        @pl.when(k - lag - 2 >= 0)
        def _():
            finish(k - lag - 2)

        return carry

    lax.fori_loop(0, chunks + lag, turn, 0)
    for h in range(chunks + lag, heads):
        head_probs(h)
    combine(last)
    for h in range(heads):
        at = slice(h * HEAD_DIM, (h + 1) * HEAD_DIM)
        for first in range(0, length, block):
            value_out[0, first : first + block, at] = jnp.dot(
                probs[h, first : first + block, first:],
                total[first:, at].astype(jnp.bfloat16),
                preferred_element_type=jnp.float32,
            ).astype(jnp.bfloat16)
    finish(last - 1)
    finish(last)

    def sent(c, carry):
        for hop in range(tensor - 1):

            @pl.when((z - hop >= 0) & (z < tensor - 1))
            def _():
                up(c, hop).wait_send()

            @pl.when((z + hop < tensor) & (z > 0))
            def _():
                down(c, hop).wait_send()

        pair_copy(c).wait_send()
        for step in range(1, groups):
            group_copy(c, step).wait_send()
        return carry

    lax.fori_loop(0, chunks, sent, 0)


def fused(d_out, attn_out, queries, keys, out_weight, segment_ids):
    dp, tensor = lax.axis_size("dp"), lax.axis_size("tensor")
    length = attn_out.shape[1]
    features, full = out_weight.shape
    width = chunk_width(full)
    chunks = full // width
    groups = dp // 2
    owned = features // dp
    half = features // 2
    heads = features // HEAD_DIM
    bf16, f32 = jnp.bfloat16, jnp.float32
    dma = pltpu.SemaphoreType.DMA
    return pl.pallas_call(
        functools.partial(kernel, dp, tensor),
        out_shape=(
            jax.ShapeDtypeStruct((1, length, features), bf16),
            jax.ShapeDtypeStruct((owned, full), f32),
        ),
        in_specs=[pl.BlockSpec(memory_space=pl.ANY)] * 6,
        out_specs=(pl.BlockSpec(memory_space=pltpu.VMEM), pl.BlockSpec(memory_space=pltpu.VMEM)),
        scratch_shapes=[
            pltpu.VMEM((chunks, length, width), bf16),
            pltpu.VMEM((chunks, features, width), bf16),
            pltpu.VMEM((length, features), bf16),
            pltpu.VMEM((length, features), bf16),
            pltpu.VMEM((length, features), bf16),
            pltpu.VMEM((1, length), jnp.int32),
            pltpu.VMEM((features, length), bf16),
            pltpu.VMEM((2, half, length), bf16),
            pltpu.VMEM((heads, length, length), bf16),
            pltpu.VMEM((length, features), f32),
            pltpu.VMEM((chunks, half, width), bf16),
            pltpu.VMEM((chunks, half, width), bf16),
            pltpu.VMEM((chunks, half, width), f32),
            pltpu.VMEM((chunks, groups - 1, owned, width), bf16),
            pltpu.VMEM((chunks, groups - 1, owned, width), bf16),
            pltpu.VMEM((chunks, owned, width), f32),
            dma((4,)),
            dma((chunks,)),
            dma((chunks,)),
            dma((tensor - 1, chunks)),
            dma((tensor - 1, chunks)),
            dma((tensor - 1, chunks)),
            dma((tensor - 1, chunks)),
            dma((chunks,)),
            dma((chunks,)),
            dma((chunks, groups - 1)),
            dma((chunks, groups - 1)),
        ],
        compiler_params=pltpu.CompilerParams(
            collective_id=0, has_side_effects=True, vmem_limit_bytes=56 * 2**20
        ),
    )(d_out, attn_out, queries, keys, out_weight, segment_ids)


def shards(d_out, attn_out, queries, keys, out_weight, segment_ids):
    if fits_kernel(d_out, attn_out, out_weight):
        return fused(d_out, attn_out, queries, keys, out_weight, segment_ids)
    grads_local = d_out[0]
    outputs = attn_out[0]
    owned_count = out_weight.shape[0] // lax.axis_size("dp")
    gathered = lax.all_gather(grads_local, "tensor", axis=0, tiled=True)
    attn_grad = lax.dot_general(
        gathered, out_weight, (((1,), (1,)), ((), ())), preferred_element_type=jnp.float32
    ).astype(jnp.bfloat16)

    def term_rows(start, count):
        return lax.dot_general(
            outputs, gathered, (((0,), (0,)), ((), ())), preferred_element_type=jnp.float32
        )

    value_rows = value_path(queries[0], keys[0], attn_grad, segment_ids[0])
    owned_rows = reduce_bucket(term_rows, owned_count)
    return (value_rows[None], owned_rows / lax.axis_size("dp"))


def solution(mesh):
    placed = (
        P("dp", "tensor", None),
        P("dp", None, "tensor"),
        P("dp", None, "tensor"),
        P("dp", None, "tensor"),
        P("tensor", None),
        P("dp", None),
    )
    return jax.shard_map(
        shards,
        mesh=mesh,
        in_specs=placed,
        out_specs=(P("dp", None, "tensor"), P(("tensor", "dp"), None)),
        check_vma=False,
    )
```

```python
import functools

import jax
import jax.numpy as jnp
from jax import lax
from jax.experimental import pallas as pl
from jax.experimental.pallas import tpu as pltpu
from jax.sharding import PartitionSpec as P

HEAD_DIM = 128


def value_path(queries, keys, attn_grad, segment_row):
    length = queries.shape[0]
    head_count = queries.shape[1] // HEAD_DIM
    query_heads = queries.reshape(length, head_count, HEAD_DIM)
    key_heads = keys.reshape(length, head_count, HEAD_DIM)
    grad_heads = attn_grad.reshape(length, head_count, HEAD_DIM)
    block_rows = min(256, length)
    score_scale = HEAD_DIM ** (-0.5)
    position = jnp.arange(length)
    result = jnp.zeros((length, head_count, HEAD_DIM), jnp.float32)
    for first_row in range(0, length, block_rows):
        stop_row = first_row + block_rows
        scores = (
            jnp.einsum(
                "qhd,khd->hqk",
                query_heads[first_row:stop_row],
                key_heads[:stop_row],
                preferred_element_type=jnp.float32,
            )
            * score_scale
        )
        allowed = (position[first_row:stop_row, None] >= position[None, :stop_row]) & (
            segment_row[first_row:stop_row, None] == segment_row[None, :stop_row]
        )
        masked = jnp.where(allowed[None], scores, -jnp.inf)
        highest = jnp.max(masked, axis=2, keepdims=True)
        weights = jnp.where(allowed[None], jnp.exp(masked - highest), 0.0)
        probabilities = (weights / jnp.sum(weights, axis=2, keepdims=True)).astype(jnp.bfloat16)
        update = jnp.einsum(
            "hqk,qhd->khd",
            probabilities,
            grad_heads[first_row:stop_row],
            preferred_element_type=jnp.float32,
        )
        result = result.at[:stop_row].add(update)
    return result.reshape(length, head_count * HEAD_DIM).astype(jnp.bfloat16)


def reduce_bucket(term_rows, owned_count):
    return lax.psum_scatter(
        term_rows(jnp.int32(0), owned_count * lax.axis_size("dp")),
        "dp",
        scatter_dimension=0,
        tiled=True,
    )


def fits_kernel(d_out, attn_out, out_weight):
    dp, tensor = lax.axis_size("dp"), lax.axis_size("tensor")
    rows, length = d_out.shape[1], attn_out.shape[1]
    features, width = out_weight.shape
    return (
        tensor >= 2
        and dp % 2 == 0
        and 4 <= dp <= 16
        and features % (dp * 16) == 0
        and features % HEAD_DIM == 0
        and rows % 16 == 0
        and length % 128 == 0
        and length * features * 24 + length * width * 2 + features * width * 7 < 40 * 2**20
        and width % chunk_width(width) == 0
        and width // chunk_width(width) >= 3
    )


def chunk_width(width):
    return 256 if width % 256 == 0 else 128


def kernel(
    dp,
    tensor,
    d_out,
    attn_out,
    queries,
    keys,
    weight,
    segments,
    value_out,
    owned_out,
    grads,
    weights,
    outputs,
    query_buf,
    key_buf,
    segment_buf,
    turned,
    flipped,
    probs,
    total,
    pair_send,
    pair_recv,
    kept,
    group_send,
    group_recv,
    mine,
    load_sem,
    grad_sem,
    weight_sem,
    up_send,
    up_recv,
    down_send,
    down_recv,
    pair_send_sem,
    pair_recv_sem,
    group_send_sem,
    group_recv_sem,
):
    chunks, length, width = grads.shape
    rows = length // tensor
    features = weight.shape[0]
    owned = features // dp
    groups = dp // 2
    heads = features // HEAD_DIM
    z = lax.axis_index("tensor")
    d = lax.axis_index("dp")
    core = lax.rem(d, 2)
    group = d // 2
    sibling = 2 * group + 1 - core
    last = chunks - 1

    def columns(c):
        return pl.ds(pl.multiple_of(c * width, width), width)

    def grad_rows(s):
        return pl.ds(pl.multiple_of(s * rows, rows), rows)

    def block_rows(g):
        return pl.ds(pl.multiple_of(g * owned, owned), owned)

    def load_grad(c):
        return pltpu.make_async_copy(
            d_out.at[0, :, columns(c)], grads.at[c, grad_rows(z), :], grad_sem.at[c]
        )

    def load_weight(c):
        return pltpu.make_async_copy(weight.at[:, columns(c)], weights.at[c], weight_sem.at[c])

    loads = [
        pltpu.make_async_copy(segments, segment_buf, load_sem.at[0]),
        pltpu.make_async_copy(queries.at[0], query_buf, load_sem.at[1]),
        pltpu.make_async_copy(keys.at[0], key_buf, load_sem.at[2]),
        pltpu.make_async_copy(attn_out.at[0], outputs, load_sem.at[3]),
    ]

    def start_grad(c, carry):
        load_grad(c).start()
        return carry

    def start_weight(c, carry):
        load_weight(c).start()
        return carry

    barrier = pltpu.get_barrier_semaphore()

    @pl.when(z > 0)
    def _():
        pl.semaphore_signal(barrier, inc=1, device_id={"tensor": z - 1}, device_id_type=pl.DeviceIdType.MESH)

    @pl.when(z < tensor - 1)
    def _():
        pl.semaphore_signal(barrier, inc=1, device_id={"tensor": z + 1}, device_id_type=pl.DeviceIdType.MESH)

    pl.semaphore_signal(barrier, inc=1, device_id={"dp": sibling}, device_id_type=pl.DeviceIdType.MESH)
    for step in range(1, groups):
        peer = 2 * lax.rem(group + step, groups) + core
        pl.semaphore_signal(barrier, inc=1, device_id={"dp": peer}, device_id_type=pl.DeviceIdType.MESH)

    pl.semaphore_wait(barrier, groups + jnp.minimum(z, 1) + jnp.minimum(tensor - 1 - z, 1))

    def up(c, hop):
        piece = grads.at[c, grad_rows(z - hop), :]
        return pltpu.make_async_remote_copy(
            src_ref=d_out.at[0, :, columns(c)] if hop == 0 else piece,
            dst_ref=piece,
            send_sem=up_send.at[hop, c],
            recv_sem=up_recv.at[hop, c],
            device_id={"tensor": z + 1},
            device_id_type=pl.DeviceIdType.MESH,
        )

    def down(c, hop):
        piece = grads.at[c, grad_rows(z + hop), :]
        return pltpu.make_async_remote_copy(
            src_ref=d_out.at[0, :, columns(c)] if hop == 0 else piece,
            dst_ref=piece,
            send_sem=down_send.at[hop, c],
            recv_sem=down_recv.at[hop, c],
            device_id={"tensor": z - 1},
            device_id_type=pl.DeviceIdType.MESH,
        )

    def arrived_up(c, hop):
        piece = grads.at[c, grad_rows(z - hop - 1), :]
        return pltpu.make_async_remote_copy(
            src_ref=piece,
            dst_ref=piece,
            send_sem=up_send.at[hop, c],
            recv_sem=up_recv.at[hop, c],
            device_id={"tensor": z - 1},
            device_id_type=pl.DeviceIdType.MESH,
        )

    def arrived_down(c, hop):
        piece = grads.at[c, grad_rows(z + hop + 1), :]
        return pltpu.make_async_remote_copy(
            src_ref=piece,
            dst_ref=piece,
            send_sem=down_send.at[hop, c],
            recv_sem=down_recv.at[hop, c],
            device_id={"tensor": z + 1},
            device_id_type=pl.DeviceIdType.MESH,
        )

    def send(c, hop):
        @pl.when((z - hop >= 0) & (z < tensor - 1))
        def _():
            up(c, hop).start()

        @pl.when((z + hop < tensor) & (z > 0))
        def _():
            down(c, hop).start()

    def send_own(c):
        send(c, 0)

    def receive(c, hop):
        @pl.when(z - hop - 1 >= 0)
        def _():
            arrived_up(c, hop).wait_recv()
            if hop + 1 < tensor - 1:

                @pl.when(z < tensor - 1)
                def _():
                    up(c, hop + 1).start()

        @pl.when(z + hop + 1 < tensor)
        def _():
            arrived_down(c, hop).wait_recv()
            if hop + 1 < tensor - 1:

                @pl.when(z > 0)
                def _():
                    down(c, hop + 1).start()

    def pair_copy(c):
        return pltpu.make_async_remote_copy(
            src_ref=pair_send.at[c],
            dst_ref=pair_recv.at[c],
            send_sem=pair_send_sem.at[c],
            recv_sem=pair_recv_sem.at[c],
            device_id={"dp": sibling},
            device_id_type=pl.DeviceIdType.MESH,
        )

    def group_copy(c, step):
        peer = 2 * lax.rem(group + step, groups) + core
        return pltpu.make_async_remote_copy(
            src_ref=group_send.at[c, step - 1],
            dst_ref=group_recv.at[c, step - 1],
            send_sem=group_send_sem.at[c, step - 1],
            recv_sem=group_recv_sem.at[c, step - 1],
            device_id={"dp": peer},
            device_id_type=pl.DeviceIdType.MESH,
        )

    ahead = min(3, chunks)
    for c in range(ahead):
        send_own(c)

    for load in loads:
        load.start()
    lax.fori_loop(0, chunks, start_grad, 0)
    lax.fori_loop(0, chunks, start_weight, 0)
    for load in loads:
        load.wait()
    turned[...] = outputs[...].T
    for part in range(2):
        owner_core = 1 - core if part == 0 else core
        for g in range(groups):
            flipped[part, g * owned : (g + 1) * owned, :] = turned[block_rows(2 * g + owner_core), :]
    total[...] = jnp.zeros_like(total)

    block = min(256, length)
    ids = segment_buf[...].astype(jnp.float32)
    ids_down = jnp.broadcast_to(ids, (128, length)).T[:, :1]

    def head_probs(h):
        at = pl.ds(pl.multiple_of(h * HEAD_DIM, HEAD_DIM), HEAD_DIM)
        for first in range(0, length, block):
            stop = first + block
            scores = lax.dot_general(
                key_buf[:stop, at],
                query_buf[first:stop, at],
                (((1,), (1,)), ((), ())),
                preferred_element_type=jnp.float32,
            ) * (HEAD_DIM ** (-0.5))
            key_at = lax.broadcasted_iota(jnp.int32, (stop, block), 0)
            query_at = first + lax.broadcasted_iota(jnp.int32, (stop, block), 1)
            allowed = (key_at <= query_at) & (ids_down[:stop] == ids[:, first:stop])
            masked = jnp.where(allowed, scores, -jnp.inf)
            highest = jnp.max(masked, axis=0, keepdims=True)
            terms = jnp.exp(masked - highest)
            probs[h, :stop, first:stop] = (
                terms * (1.0 / jnp.sum(terms, axis=0, keepdims=True))
            ).astype(jnp.bfloat16)

    def multiply(c):
        load_weight(c).wait()
        load_grad(c).wait()
        grad = grads[c]
        pair_send[c] = jnp.dot(flipped[0], grad, preferred_element_type=jnp.float32).astype(jnp.bfloat16)
        pair_copy(c).start()
        kept[c] = jnp.dot(flipped[1], grad, preferred_element_type=jnp.float32)
        total[...] += lax.dot_general(
            grad, weights[c], (((1,), (1,)), ((), ())), preferred_element_type=jnp.float32
        )

    def combine(c):
        pair_copy(c).wait_recv()
        for step in range(1, groups):
            at = block_rows(lax.rem(group + step, groups))
            group_send[c, step - 1] = (kept[c, at, :] + pair_recv[c, at, :].astype(jnp.float32)).astype(jnp.bfloat16)
            group_copy(c, step).start()
        at = block_rows(group)
        mine[c] = kept[c, at, :] + pair_recv[c, at, :].astype(jnp.float32)

    def finish(c):
        result = mine[c]
        for step in range(1, groups):
            group_copy(c, step).wait_recv()
            result += group_recv[c, step - 1].astype(jnp.float32)
        owned_out[:, columns(c)] = result / dp

    lag = tensor - 2

    def turn(k, carry):
        for hop in range(tensor - 1):
            c = k - hop

            @pl.when((c >= 0) & (c < chunks))
            def _():
                receive(c, hop)

        @pl.when(k + ahead < chunks)
        def _():
            send_own(k + ahead)

        @pl.when(k - lag >= 0)
        def _():
            multiply(k - lag)

        @pl.when(k - lag - 1 >= 0)
        def _():
            combine(k - lag - 1)

        @pl.when(k - lag - 3 >= 0)
        def _():
            finish(k - lag - 3)

        @pl.when(k < heads)
        def _():
            head_probs(k)

        return carry

    lax.fori_loop(0, chunks + lag, turn, 0)
    for h in range(chunks + lag, heads):
        head_probs(h)
    combine(last)
    for h in range(heads):
        at = slice(h * HEAD_DIM, (h + 1) * HEAD_DIM)
        for first in range(0, length, block):
            value_out[0, first : first + block, at] = jnp.dot(
                probs[h, first : first + block, first:],
                total[first:, at].astype(jnp.bfloat16),
                preferred_element_type=jnp.float32,
            ).astype(jnp.bfloat16)
    finish(last - 2)
    finish(last - 1)
    finish(last)

    def sent(c, carry):
        for hop in range(tensor - 1):

            @pl.when((z - hop >= 0) & (z < tensor - 1))
            def _():
                up(c, hop).wait_send()

            @pl.when((z + hop < tensor) & (z > 0))
            def _():
                down(c, hop).wait_send()

        pair_copy(c).wait_send()
        for step in range(1, groups):
            group_copy(c, step).wait_send()
        return carry

    lax.fori_loop(0, chunks, sent, 0)


def hand_on(values, sums, value_out, owned_out, value_buf, owned_buf, load_sem, store_sem):
    parts = load_sem.shape[1]
    loads, stores = [], []
    for index, (source, middle, target, dim) in enumerate(
        ((values, value_buf, value_out, 1), (sums, owned_buf, owned_out, 0))
    ):
        step = source.shape[dim] // parts
        for part in range(parts):
            at = (slice(None),) * dim + (pl.ds(part * step, step),)
            loads.append(pltpu.make_async_copy(source.at[at], middle.at[at], load_sem.at[index, part]))
            stores.append(pltpu.make_async_copy(middle.at[at], target.at[at], store_sem.at[index, part]))
    for load in loads:
        load.start()
    for load, store in zip(loads, stores):
        load.wait()
        store.start()
    for store in stores:
        store.wait()


def deliver(values, sums):
    parts = 2 if values.shape[1] % 32 == 0 and sums.shape[0] % 16 == 0 else 1
    dma = pltpu.SemaphoreType.DMA
    return pl.pallas_call(
        hand_on,
        out_shape=(
            jax.ShapeDtypeStruct(values.shape, values.dtype),
            jax.ShapeDtypeStruct(sums.shape, sums.dtype),
        ),
        in_specs=[pl.BlockSpec(memory_space=pl.ANY)] * 2,
        out_specs=(pl.BlockSpec(memory_space=pl.ANY),) * 2,
        scratch_shapes=[
            pltpu.VMEM(values.shape, values.dtype),
            pltpu.VMEM(sums.shape, sums.dtype),
            dma((2, parts)),
            dma((2, parts)),
        ],
        compiler_params=pltpu.CompilerParams(vmem_limit_bytes=60 * 2**20),
    )(values, sums)


def fused(d_out, attn_out, queries, keys, out_weight, segment_ids):
    dp, tensor = lax.axis_size("dp"), lax.axis_size("tensor")
    length = attn_out.shape[1]
    features, full = out_weight.shape
    width = chunk_width(full)
    chunks = full // width
    groups = dp // 2
    owned = features // dp
    half = features // 2
    heads = features // HEAD_DIM
    bf16, f32 = jnp.bfloat16, jnp.float32
    dma = pltpu.SemaphoreType.DMA
    values, sums = pl.pallas_call(
        functools.partial(kernel, dp, tensor),
        out_shape=(
            jax.ShapeDtypeStruct((1, length, features), bf16),
            jax.ShapeDtypeStruct((owned, full), f32),
        ),
        in_specs=[pl.BlockSpec(memory_space=pl.ANY)] * 6,
        out_specs=(pl.BlockSpec(memory_space=pltpu.VMEM), pl.BlockSpec(memory_space=pltpu.VMEM)),
        scratch_shapes=[
            pltpu.VMEM((chunks, length, width), bf16),
            pltpu.VMEM((chunks, features, width), bf16),
            pltpu.VMEM((length, features), bf16),
            pltpu.VMEM((length, features), bf16),
            pltpu.VMEM((length, features), bf16),
            pltpu.VMEM((1, length), jnp.int32),
            pltpu.VMEM((features, length), bf16),
            pltpu.VMEM((2, half, length), bf16),
            pltpu.VMEM((heads, length, length), bf16),
            pltpu.VMEM((length, features), f32),
            pltpu.VMEM((chunks, half, width), bf16),
            pltpu.VMEM((chunks, half, width), bf16),
            pltpu.VMEM((chunks, half, width), f32),
            pltpu.VMEM((chunks, groups - 1, owned, width), bf16),
            pltpu.VMEM((chunks, groups - 1, owned, width), bf16),
            pltpu.VMEM((chunks, owned, width), f32),
            dma((4,)),
            dma((chunks,)),
            dma((chunks,)),
            dma((tensor - 1, chunks)),
            dma((tensor - 1, chunks)),
            dma((tensor - 1, chunks)),
            dma((tensor - 1, chunks)),
            dma((chunks,)),
            dma((chunks,)),
            dma((chunks, groups - 1)),
            dma((chunks, groups - 1)),
        ],
        compiler_params=pltpu.CompilerParams(
            collective_id=0, has_side_effects=True, vmem_limit_bytes=56 * 2**20
        ),
    )(d_out, attn_out, queries, keys, out_weight, segment_ids)
    return deliver(values, sums)


def shards(d_out, attn_out, queries, keys, out_weight, segment_ids):
    if fits_kernel(d_out, attn_out, out_weight):
        return fused(d_out, attn_out, queries, keys, out_weight, segment_ids)
    grads_local = d_out[0]
    outputs = attn_out[0]
    owned_count = out_weight.shape[0] // lax.axis_size("dp")
    gathered = lax.all_gather(grads_local, "tensor", axis=0, tiled=True)
    attn_grad = lax.dot_general(
        gathered, out_weight, (((1,), (1,)), ((), ())), preferred_element_type=jnp.float32
    ).astype(jnp.bfloat16)

    def term_rows(start, count):
        return lax.dot_general(
            outputs, gathered, (((0,), (0,)), ((), ())), preferred_element_type=jnp.float32
        )

    value_rows = value_path(queries[0], keys[0], attn_grad, segment_ids[0])
    owned_rows = reduce_bucket(term_rows, owned_count)
    return (value_rows[None], owned_rows / lax.axis_size("dp"))


def solution(mesh):
    placed = (
        P("dp", "tensor", None),
        P("dp", None, "tensor"),
        P("dp", None, "tensor"),
        P("dp", None, "tensor"),
        P("tensor", None),
        P("dp", None),
    )
    return jax.shard_map(
        shards,
        mesh=mesh,
        in_specs=placed,
        out_specs=(P("dp", None, "tensor"), P(("tensor", "dp"), None)),
        check_vma=False,
    )
```
